1024 devices in a mesh: dp: 32 (over z), dom: 2 (over x_hi), mp: 16 (over x_lo, y, core).
Axes of the slice: x: 4 (x_hi: 2, x_lo: 2; x = x_hi * 2 + x_lo), y: 4, z: 32, core: 2. Of those that a mesh axis runs over, the one named last changes fastest.
Arguments:
- img_embed: bfloat16 [16384, 1152], P('dp'), may hold values from -43 to 43
- txt_embed: bfloat16 [16384, 1152], P(('dom', 'mp')), may hold values from -43 to 43
- img_feats: bfloat16 [16384, 1152], P('dp'), may hold values from -6 to 6
- txt_feats: bfloat16 [16384, 1152], P(('dom', 'mp')), may hold values from -6 to 6
- img_ids: int32 [16384], P('dp'), may hold values from 0 to 2047, as said below
- txt_ids: int32 [16384], P(('dom', 'mp')), may hold values from 0 to 2047
- loss_params: float32 [3], replicated, as said below
Outputs:
- img_weight_grad: float32 [1152, 1152], P('dp', ('dom', 'mp'))
- txt_weight_grad: float32 [1152, 1152], P(('dom', 'mp'), 'dp')
The draws below stay inside these ranges and needn't reach their ends.
Inputs may be any that keep to these rules, and one draw needn't show every extreme that they name: `img_ids`: an image row and a text row form a positive pair exactly when their labels are equal. `loss_params`: entry 0 is the logit scale in 8 to 14, entry 1 the logit bias in -6 to -2, entry 2 the cotangent, positive.
All inputs are finite; a program needn't handle non-finite values.
Results may differ from the reference program's by a relative error of at most 0.0035.
Values may be sent and summed in bfloat16 or wider, within the bound.
No kernel may reach another device: no remote copies, remote signals or barrier semaphores. Data moves between devices by JAX's collectives and lax.ppermute only.
A program may use at most 32 MiB of HBM per device.

```python
import jax
import jax.numpy as jnp
from jax import lax

FEATURES = 1152
EMBED_DIM = 1152
IMG_ROWS = 512
PAIRS_ALL = 16384
N_DP = 32


def draw_labels(key):
    image_labels = jax.random.randint(jax.random.fold_in(key, 11), (PAIRS_ALL,), 0, PAIRS_ALL // 8)
    text_labels = jax.random.randint(jax.random.fold_in(key, 12), (PAIRS_ALL,), 0, PAIRS_ALL // 8)
    return (image_labels, text_labels)


def draw_centres(key):
    return jax.random.truncated_normal(jax.random.fold_in(key, 13), -4.0, 4.0, (PAIRS_ALL // 8, EMBED_DIM), jnp.float32)


def draw_img_ids(key, part):
    return draw_labels(key)[0]


def draw_txt_ids(key, part):
    return draw_labels(key)[1]


def draw_img_embed(key, part):
    labels = draw_labels(key)[0]
    centres = draw_centres(key)
    key = jax.random.fold_in(key, 21)
    shared = centres[labels]
    jitter = jax.random.truncated_normal(key, -4.0, 4.0, (PAIRS_ALL, EMBED_DIM), jnp.float32)
    return (0.8 * shared + 0.6 * jitter).astype(jnp.bfloat16)


def draw_txt_embed(key, part):
    labels = draw_labels(key)[1]
    centres = draw_centres(key)
    key = jax.random.fold_in(key, 22)
    shared = centres[labels]
    jitter = jax.random.truncated_normal(key, -4.0, 4.0, (PAIRS_ALL, EMBED_DIM), jnp.float32)
    return (0.8 * shared + 0.6 * jitter).astype(jnp.bfloat16)


def draw_loss_params(key, part):
    key = jax.random.fold_in(key, 31)
    values = jax.random.uniform(key, (3,), jnp.float32)
    scale_t = 8.0 + 6.0 * values[0]
    shift_b = -6.0 + 4.0 * values[1]
    cotangent = (0.5 + 1.5 * values[2]) * (EMBED_DIM * PAIRS_ALL ** 0.5 / 240.0)
    return jnp.stack([scale_t, shift_b, cotangent]).astype(jnp.float32)


def steps_of(stream_key, extent, cuts, smallest, high):
    factor_of, own = 1.0, jax.random.fold_in(stream_key, 6)
    for dim, shards_of in cuts:
        heights = jnp.exp(jax.random.uniform(jax.random.fold_in(own, dim), (shards_of,), jnp.float32, smallest / len(cuts), high / len(cuts)))
        factor_of = factor_of * jnp.repeat(heights, extent[dim] // shards_of).reshape([-1 if axis == dim else 1 for axis in range(len(extent))])
    return factor_of


def bell_draw(own_key, shape, deviation, most, cuts=(), dtype=jnp.bfloat16):
    level = steps_of(own_key, shape, cuts, -0.22, 0.18) if cuts else 1.0
    entries = jax.random.normal(own_key, shape, jnp.float32) * deviation * level
    return jnp.minimum(jnp.maximum(entries, -most), most).astype(dtype)


def setup_inputs(seed: int = 0) -> dict:
    keys = jax.random.split(jax.random.key(seed), 8)
    img_embed = draw_img_embed(jax.random.fold_in(keys[7], 71), 0)
    txt_embed = draw_txt_embed(jax.random.fold_in(keys[7], 71), 0)
    img_feats = bell_draw(keys[2], (PAIRS_ALL, FEATURES), 1.0, 6.0, ((0, 32),))
    txt_feats = bell_draw(keys[3], (PAIRS_ALL, FEATURES), 1.0, 6.0, ((0, 32),))
    img_ids = draw_img_ids(jax.random.fold_in(keys[7], 71), 0)
    txt_ids = draw_txt_ids(jax.random.fold_in(keys[7], 71), 0)
    loss_params = draw_loss_params(jax.random.fold_in(keys[7], 71), 0)
    return dict(img_embed=img_embed, txt_embed=txt_embed, img_feats=img_feats, txt_feats=txt_feats, img_ids=img_ids, txt_ids=txt_ids, loss_params=loss_params)


def unit_rows(embedded):
    values = embedded.astype(jnp.float32)
    length = jnp.sqrt(lax.optimization_barrier(jnp.sum(values * values, axis=1, keepdims=True)) + 1e-06)
    return ((values / length).astype(jnp.bfloat16), length)

def reference(img_embed, txt_embed, img_feats, txt_feats, img_ids, txt_ids, loss_params):
    img_unit, img_length = unit_rows(img_embed)
    txt_unit, txt_length = unit_rows(txt_embed)
    scale_t = loss_params[0]
    shift_b = loss_params[1]
    cotangent = loss_params[2]
    factor = -cotangent / PAIRS_ALL
    unit_blocks = img_unit.reshape(N_DP, IMG_ROWS, EMBED_DIM)
    label_blocks = img_ids.reshape(N_DP, IMG_ROWS)

    def one_block(running, inputs):
        unit_block, label_block = inputs
        similar = lax.dot_general(unit_block, txt_unit, (((1,), (1,)), ((), ())), preferred_element_type=jnp.float32)
        pair_sign = jnp.where(label_block[:, None] == txt_ids[None, :], 1.0, -1.0).astype(jnp.float32)
        logits = scale_t * similar + shift_b
        weights = (scale_t * factor * pair_sign * jax.nn.sigmoid(-pair_sign * logits)).astype(jnp.bfloat16)
        image_part = jnp.dot(weights, txt_unit, preferred_element_type=jnp.float32)
        text_part = lax.dot_general(weights, unit_block, (((0,), (0,)), ((), ())), preferred_element_type=jnp.float32)
        return (running + text_part, image_part)
    start_text = jnp.zeros((PAIRS_ALL, EMBED_DIM), jnp.float32)
    txt_grad, image_parts = lax.scan(one_block, start_text, (unit_blocks, label_blocks))
    img_grad = image_parts.reshape(PAIRS_ALL, EMBED_DIM)
    img_values = img_unit.astype(jnp.float32)
    txt_values = txt_unit.astype(jnp.float32)
    img_radial = lax.optimization_barrier(jnp.sum(img_values * img_grad, axis=1, keepdims=True))
    txt_radial = lax.optimization_barrier(jnp.sum(txt_values * txt_grad, axis=1, keepdims=True))
    img_dz = ((img_grad - img_values * img_radial) / img_length).astype(jnp.bfloat16)
    txt_dz = ((txt_grad - txt_values * txt_radial) / txt_length).astype(jnp.bfloat16)
    img_weight_grad = lax.dot_general(img_feats, img_dz, (((0,), (0,)), ((), ())), preferred_element_type=jnp.float32)
    txt_weight_grad = lax.dot_general(txt_feats, txt_dz, (((0,), (0,)), ((), ())), preferred_element_type=jnp.float32)
    return (img_weight_grad, txt_weight_grad)
```

```python
import functools

import jax
import jax.numpy as jnp
import numpy as np
from jax import lax
from jax.experimental import pallas as pl
from jax.experimental.pallas import tpu as pltpu
from jax.sharding import Mesh
from jax.sharding import PartitionSpec as P

F32 = jnp.float32
BF16 = jnp.bfloat16
TN = (((0,), (0,)), ((), ()))
NT = (((1,), (1,)), ((), ()))
VMEM_LIMIT = 56 * 1024 * 1024


def unit_rows(embedded):
    values = embedded.astype(F32)
    length = jnp.sqrt(jnp.sum(values * values, axis=1, keepdims=True) + 1e-06)
    inverse = 1.0 / length
    return (values * inverse).astype(BF16), inverse


def partial_kernel(
    n_chips,
    pad,
    pairs_total,
    core_ref,
    params_ref,
    img_ref,
    txt_ref,
    feats_ref,
    img_ids_ref,
    txt_ids_ref,
    mine_ref,
    other_ref,
    image_ref,
    text_ref,
):
    width = feats_ref.shape[1]
    block = width // (2 * n_chips)
    scale_t = params_ref[0]
    shift_b = params_ref[1]
    factor = scale_t * (-params_ref[2] / pairs_total)
    img_unit, img_inverse = unit_rows(img_ref[...])
    txt_unit, txt_inverse = unit_rows(txt_ref[...])
    similar = lax.dot_general(img_unit, txt_unit, NT, preferred_element_type=F32)
    logits = scale_t * similar + shift_b
    same = img_ids_ref[...] == txt_ids_ref[...]
    minus = jnp.where(same, logits, -logits)
    weights = (jnp.where(same, factor, -factor) / (1.0 + jnp.exp(minus))).astype(BF16)
    img_radial = jnp.sum(weights.astype(F32) * similar, axis=1, keepdims=True)
    img_grad = jnp.dot(weights, txt_unit, preferred_element_type=F32)
    img_grad = (img_grad - img_unit.astype(F32) * img_radial) * img_inverse
    image_ref[0:width, :] = img_grad.T
    txt_grad = lax.dot_general(weights, img_unit, TN, preferred_element_type=F32)
    txt_values = txt_unit.astype(F32)
    txt_radial = jnp.sum(txt_grad * txt_values, axis=1, keepdims=True)
    txt_grad = (txt_grad - txt_values * txt_radial) * txt_inverse
    high = txt_grad.astype(BF16)
    low = (txt_grad - high.astype(F32)).astype(BF16)
    feats = feats_ref[...]
    text_ref[0:width, :] = lax.dot_general(
        feats, high, TN, preferred_element_type=F32
    ) + lax.dot_general(feats, low, TN, preferred_element_type=F32)
    image_ref[width:, :] = jnp.zeros_like(image_ref[width:, :])
    text_ref[width:, :] = jnp.zeros_like(text_ref[width:, :])
    me = core_ref[0]
    for core in range(2):

        @pl.when(me == core)
        def _():
            for chip in range(n_chips):
                for kept, ref in ((core, mine_ref), (1 - core, other_ref)):
                    start = (2 * chip + kept) * block
                    ref[chip, :, 0:width] = text_ref[start : start + pad, :].astype(ref.dtype)
                    ref[chip, :, width:] = image_ref[start : start + pad, :].astype(ref.dtype)


def project_kernel(n_loop, block, parts_ref, feats_ref, out_ref, rows_ref):
    n_parts = parts_ref.shape[0]
    width = feats_ref.shape[1]
    total = parts_ref[0].astype(F32)
    for part in range(1, n_parts):
        total = total + parts_ref[part].astype(F32)
    text = total[0:block, 0:width]
    image = total[:, width:]
    high = image.astype(BF16)
    low = (image - high.astype(F32)).astype(BF16)
    feats = feats_ref[...]
    projected = jnp.dot(high, feats, preferred_element_type=F32) + jnp.dot(
        low, feats, preferred_element_type=F32
    )
    both = jnp.concatenate(
        [projected[0:block], text, jnp.zeros((128 - 2 * block, width), F32)], axis=0
    )
    rows_ref[...] = both.T
    first = out_ref.shape[1]
    rest = block - first
    lane = lax.broadcasted_iota(jnp.int32, (rest, 128), 1)
    for target in range(n_loop):
        top = rows_ref[target * block : target * block + first, :]
        bottom = rows_ref[target * block + first : (target + 1) * block, :]
        image_bottom = pltpu.roll(bottom, 2 * block, 1)
        text_bottom = pltpu.roll(bottom, block, 1)
        tail = jnp.concatenate([image_bottom, text_bottom], axis=0)
        lanes = lax.broadcasted_iota(jnp.int32, (first, 128), 1)
        out_ref[target] = jnp.where(lanes < 2 * block, top, tail).astype(out_ref.dtype)


def total_kernel(block, parts_ref, img_ref, txt_ref):
    total = parts_ref[0].astype(F32)
    for part in range(1, parts_ref.shape[0]):
        total = total + parts_ref[part].astype(F32)
    first = parts_ref.shape[1]
    rest = block - first
    image_bottom = pltpu.roll(total, 128 - 2 * block, 1)[0:rest]
    text_bottom = pltpu.roll(total, 128 - block, 1)[rest : 2 * rest]
    lane = lax.broadcasted_iota(jnp.int32, (rest, 128), 1)
    bottom = jnp.where(lane < block, image_bottom, text_bottom)
    whole = jnp.concatenate([total, bottom, jnp.zeros((128 - block, 128), F32)], axis=0)
    img_ref[...] = whole[0:block, 0:block]
    txt_ref[...] = whole.T[block : 2 * block, 0:block]


def whole_spec():
    return pl.BlockSpec(memory_space=pltpu.VMEM)


def scalar_spec():
    return pl.BlockSpec(memory_space=pltpu.SMEM)


def compiler_params():
    return pltpu.CompilerParams(vmem_limit_bytes=VMEM_LIMIT)


def per_device(img_embed, txt_embed, img_feats, txt_feats, img_ids, txt_ids, loss_params):
    n_loop = lax.axis_size("dp")
    n_chips = lax.axis_size(("dom", "chip"))
    rows, width = img_embed.shape
    block = width // n_loop
    pad = -(-block // 8) * 8
    core = lax.axis_index("core").astype(jnp.int32).reshape(1)
    lanes = width + rows
    shape = (n_chips, pad, lanes)
    mine, other = pl.pallas_call(
        functools.partial(partial_kernel, n_chips, pad, float(rows * n_loop)),
        out_shape=(jax.ShapeDtypeStruct(shape, F32), jax.ShapeDtypeStruct(shape, BF16)),
        in_specs=[scalar_spec(), scalar_spec()] + [whole_spec()] * 5,
        out_specs=[whole_spec()] * 2,
        scratch_shapes=[
            pltpu.VMEM((width + 8, rows), F32),
            pltpu.VMEM((width + 8, width), F32),
        ],
        compiler_params=compiler_params(),
        name="partial_gradients",
    )(
        core,
        loss_params,
        img_embed,
        txt_embed,
        txt_feats,
        img_ids.reshape(rows, 1),
        txt_ids.reshape(1, -1),
    )
    theirs = lax.ppermute(other, "core", [(0, 1), (1, 0)])
    chip_sum = (mine + theirs.astype(F32)).astype(BF16)
    parts = lax.all_to_all(chip_sum, ("dom", "chip"), split_axis=0, concat_axis=0, tiled=True)
    blocks = pl.pallas_call(
        functools.partial(project_kernel, n_loop, block),
        out_shape=jax.ShapeDtypeStruct((n_loop, 2 * block // 3, 128), BF16),
        in_specs=[whole_spec()] * 2,
        out_specs=whole_spec(),
        scratch_shapes=[pltpu.VMEM((width, 128), F32)],
        compiler_params=compiler_params(),
        name="project_blocks",
    )(parts, img_feats)
    loop_parts = lax.all_to_all(blocks, "dp", split_axis=0, concat_axis=0, tiled=True)
    return pl.pallas_call(
        functools.partial(total_kernel, block),
        out_shape=(jax.ShapeDtypeStruct((block, block), F32),) * 2,
        in_specs=[whole_spec()],
        out_specs=[whole_spec()] * 2,
        compiler_params=compiler_params(),
        name="sum_blocks",
    )(loop_parts)


def solution(mesh):
    shape = mesh.shape
    devices = np.asarray(mesh.devices).reshape(shape["dp"], shape["dom"], shape["mp"] // 2, 2)
    mesh = Mesh(devices, ("dp", "dom", "chip", "core"))
    plane = ("dom", "chip", "core")
    return jax.shard_map(
        per_device,
        mesh=mesh,
        in_specs=(
            P("dp", None),
            P(plane, None),
            P("dp", None),
            P(plane, None),
            P("dp"),
            P(plane),
            P(),
        ),
        out_specs=(P("dp", plane), P(plane, "dp")),
        check_vma=False,
    )
```

```python
import functools

import jax
import jax.numpy as jnp
import numpy as np
from jax import lax
from jax.experimental import pallas as pl
from jax.experimental.pallas import tpu as pltpu
from jax.sharding import Mesh
from jax.sharding import PartitionSpec as P

F32 = jnp.float32
BF16 = jnp.bfloat16
TN = (((0,), (0,)), ((), ()))
NT = (((1,), (1,)), ((), ()))


def unit_rows(embedded):
    values = embedded.astype(F32)
    length = jnp.sqrt(jnp.sum(values * values, axis=1, keepdims=True) + 1e-06)
    inverse = 1.0 / length
    return (values * inverse).astype(BF16), inverse


def partial_kernel(
    n_chips,
    pairs_total,
    core_ref,
    params_hbm,
    img_hbm,
    txt_hbm,
    feats_hbm,
    img_ids_hbm,
    txt_ids_hbm,
    mine_ref,
    other_ref,
    grads_ref,
    params_ref,
    img_ref,
    txt_ref,
    feats_ref,
    img_ids_ref,
    txt_ids_ref,
    sems,
):
    copies = []
    for number, (source, target) in enumerate(
        (
            (img_hbm, img_ref),
            (txt_hbm, txt_ref),
            (img_ids_hbm, img_ids_ref),
            (txt_ids_hbm, txt_ids_ref),
            (params_hbm, params_ref),
            (feats_hbm, feats_ref),
        )
    ):
        copies.append(pltpu.make_async_copy(source, target, sems.at[number]))
        copies[-1].start()
    rows = img_ref.shape[0]
    width = feats_ref.shape[1]
    pair = width // n_chips
    block = pair // 2
    body = block // 8 * 8
    n_tiles = (width + rows) // 128
    copies[0].wait()
    img_unit, img_inverse = unit_rows(img_ref[...])
    copies[1].wait()
    txt_unit, txt_inverse = unit_rows(txt_ref[...])
    for copy in copies[2:5]:
        copy.wait()
    scale_t = params_ref[0]
    shift_b = params_ref[1]
    factor = scale_t * (-params_ref[2] / pairs_total)
    similar = lax.dot_general(img_unit, txt_unit, NT, preferred_element_type=F32)
    logits = scale_t * similar + shift_b
    img_ids = jnp.broadcast_to(img_ids_ref[...], (8, rows)).T[:, 0:1]
    same = img_ids == txt_ids_ref[...]
    minus = jnp.where(same, logits, -logits)
    weights = (jnp.where(same, factor, -factor) / (1.0 + jnp.exp(minus))).astype(BF16)
    img_radial = jnp.sum(weights.astype(F32) * similar, axis=1, keepdims=True)
    img_grad = jnp.dot(weights, txt_unit, preferred_element_type=F32)
    img_grad = (img_grad - img_unit.astype(F32) * img_radial) * img_inverse
    grads_ref[:, width:] = img_grad.T
    txt_grad = lax.dot_general(weights, img_unit, TN, preferred_element_type=F32)
    txt_values = txt_unit.astype(F32)
    txt_radial = jnp.sum(txt_grad * txt_values, axis=1, keepdims=True)
    txt_grad = ((txt_grad - txt_values * txt_radial) * txt_inverse).astype(BF16)
    copies[5].wait()
    grads_ref[:, 0:width] = lax.dot_general(
        feats_ref[...], txt_grad, TN, preferred_element_type=F32
    )
    me = core_ref[0]
    low_half = lax.broadcasted_iota(jnp.int32, (8, 128), 0) < 4
    for core in range(2):

        @pl.when(me == core)
        def _():
            for chip in range(n_chips):
                shared = grads_ref[pair * chip + body : pair * chip + body + 8, :]
                turned = pltpu.roll(shared, 4, 0)
                for kept, ref in ((core, mine_ref), (1 - core, other_ref)):
                    start = pair * chip + (body + 8) * kept
                    whole = grads_ref[start : start + body, :].astype(ref.dtype)
                    even, odd = (turned, shared) if kept else (shared, turned)
                    for tile in range(n_tiles):
                        ref[chip, body * tile : body * (tile + 1), :] = whole[
                            :, 128 * tile : 128 * (tile + 1)
                        ]
                    ends = []
                    for tile in range(0, n_tiles, 2):
                        last = min(tile + 1, n_tiles - 1)
                        ends.append(
                            jnp.where(
                                low_half,
                                even[:, 128 * tile : 128 * (tile + 1)],
                                odd[:, 128 * last : 128 * (last + 1)],
                            )
                        )
                    ref[chip, body * n_tiles :, :] = jnp.concatenate(ends, axis=0).astype(ref.dtype)


def project_kernel(n_loop, block, parts_ref, feats_ref, out_ref, rows_ref, total_ref):
    n_parts = parts_ref.shape[0]
    rows, width = feats_ref.shape
    body = block // 8 * 8
    n_tiles = (width + rows) // 128
    total = parts_ref[0].astype(F32)
    for part in range(1, n_parts):
        total = total + parts_ref[part].astype(F32)
    for tile in range(n_tiles):
        columns = slice(128 * tile, 128 * (tile + 1))
        total_ref[0:body, columns] = total[body * tile : body * (tile + 1)]
        start = body * n_tiles + 8 * (tile // 2)
        end = total[start : start + 8]
        total_ref[body : body + 8, columns] = pltpu.roll(end, 4, 0) if tile % 2 else end
    text = total_ref[0:block, 0:width]
    image = total_ref[:, width:]
    high = image.astype(BF16)
    low = (image - high.astype(F32)).astype(BF16)
    feats = feats_ref[...]
    projected = jnp.dot(high, feats, preferred_element_type=F32) + jnp.dot(
        low, feats, preferred_element_type=F32
    )
    both = jnp.concatenate(
        [projected[0:block], text, jnp.zeros((128 - 2 * block, width), F32)], axis=0
    )
    rows_ref[...] = both.T
    first = out_ref.shape[1]
    rest = block - first
    lane = lax.broadcasted_iota(jnp.int32, (first, 128), 1)
    for target in range(n_loop):
        top = rows_ref[target * block : target * block + first, :]
        bottom = rows_ref[target * block + first : (target + 1) * block, :]
        tail = jnp.concatenate(
            [pltpu.roll(bottom, 2 * block, 1), pltpu.roll(bottom, block, 1)], axis=0
        )
        out_ref[target] = jnp.where(lane < 2 * block, top, tail).astype(out_ref.dtype)


def total_kernel(block, core_ref, parts_ref, img_ref, txt_ref):
    total = parts_ref[0].astype(F32)
    for part in range(1, parts_ref.shape[0]):
        total = total + parts_ref[part].astype(F32)
    first = parts_ref.shape[1]
    rest = block - first
    extra = block % 8
    image_bottom = pltpu.roll(total, 128 - 2 * block, 1)[0:rest]
    text_bottom = pltpu.roll(total, 128 - block, 1)[rest : 2 * rest]
    lane = lax.broadcasted_iota(jnp.int32, (rest, 128), 1)
    bottom = jnp.where(lane < block, image_bottom, text_bottom)
    whole = jnp.concatenate([total, bottom, jnp.zeros((128 - block, 128), F32)], axis=0)
    place = lax.broadcasted_iota(jnp.int32, whole.shape, 1)
    inside = jnp.where(place < block, place, place - block)
    ordered = jnp.where(
        inside < extra, pltpu.roll(whole, 128 - (block - extra), 1), pltpu.roll(whole, extra, 1)
    )
    whole = jnp.where(core_ref[0] == 1, ordered, whole)
    img_ref[...] = whole[0:block, 0:block]
    txt_ref[...] = whole.T[block : 2 * block, 0:block]


def whole_spec():
    return pl.BlockSpec(memory_space=pltpu.VMEM)


def scalar_spec():
    return pl.BlockSpec(memory_space=pltpu.SMEM)


def compiler_params(mib):
    return pltpu.CompilerParams(vmem_limit_bytes=mib * 1024 * 1024)


def per_device(img_embed, txt_embed, img_feats, txt_feats, img_ids, txt_ids, loss_params):
    n_loop = lax.axis_size("dp")
    n_chips = lax.axis_size(("dom", "chip"))
    rows, width = img_embed.shape
    block = width // n_loop
    core = lax.axis_index("core").astype(jnp.int32).reshape(1)
    lanes = width + rows
    shape = (n_chips, -(-block * (lanes // 128) // 8) * 8, 128)
    mine, other = pl.pallas_call(
        functools.partial(partial_kernel, n_chips, float(rows * n_loop)),
        out_shape=(jax.ShapeDtypeStruct(shape, F32), jax.ShapeDtypeStruct(shape, BF16)),
        in_specs=[scalar_spec()] + [pl.BlockSpec(memory_space=pltpu.HBM)] * 6,
        out_specs=[whole_spec()] * 2,
        scratch_shapes=[
            pltpu.VMEM((width, lanes), F32),
            pltpu.SMEM(loss_params.shape, F32),
            pltpu.VMEM(img_embed.shape, BF16),
            pltpu.VMEM(txt_embed.shape, BF16),
            pltpu.VMEM(txt_feats.shape, BF16),
            pltpu.VMEM((1, rows), jnp.int32),
            pltpu.VMEM((1, txt_ids.shape[0]), jnp.int32),
            pltpu.SemaphoreType.DMA((6,)),
        ],
        compiler_params=compiler_params(36),
        name="partial_gradients",
    )(
        core,
        *(
            pltpu.with_memory_space_constraint(array, pltpu.HBM)
            for array in (
                loss_params,
                img_embed,
                txt_embed,
                txt_feats,
                img_ids.reshape(1, rows),
                txt_ids.reshape(1, -1),
            )
        ),
    )
    theirs = lax.ppermute(other, "core", [(0, 1), (1, 0)])
    chip_sum = (mine + theirs.astype(F32)).astype(BF16)
    parts = lax.all_to_all(chip_sum, ("dom", "chip"), split_axis=0, concat_axis=0, tiled=True)
    blocks = pl.pallas_call(
        functools.partial(project_kernel, n_loop, block),
        out_shape=jax.ShapeDtypeStruct((n_loop, 2 * block // 3, 128), BF16),
        in_specs=[whole_spec()] * 2,
        out_specs=whole_spec(),
        scratch_shapes=[
            pltpu.VMEM((width, 128), F32),
            pltpu.VMEM((block // 8 * 8 + 8, lanes), F32),
        ],
        compiler_params=compiler_params(16),
        name="project_blocks",
    )(parts, img_feats)
    loop_parts = lax.all_to_all(blocks, "dp", split_axis=0, concat_axis=0, tiled=True)
    return pl.pallas_call(
        functools.partial(total_kernel, block),
        out_shape=(jax.ShapeDtypeStruct((block, block), F32),) * 2,
        in_specs=[scalar_spec(), whole_spec()],
        out_specs=[whole_spec()] * 2,
        compiler_params=compiler_params(4),
        name="sum_blocks",
    )(core, loop_parts)


def solution(mesh):
    shape = mesh.shape
    devices = np.asarray(mesh.devices).reshape(shape["dp"], shape["dom"], shape["mp"] // 2, 2)
    mesh = Mesh(devices, ("dp", "dom", "chip", "core"))
    plane = ("dom", "chip", "core")
    return jax.shard_map(
        per_device,
        mesh=mesh,
        in_specs=(
            P("dp", None),
            P(plane, None),
            P("dp", None),
            P(plane, None),
            P("dp"),
            P(plane),
            P(),
        ),
        out_specs=(P("dp", plane), P(plane, "dp")),
        check_vma=False,
    )
```

```python
import functools

import jax
import jax.numpy as jnp
import numpy as np
from jax import lax
from jax.experimental import pallas as pl
from jax.experimental.pallas import tpu as pltpu
from jax.sharding import Mesh
from jax.sharding import PartitionSpec as P

F32 = jnp.float32
BF16 = jnp.bfloat16
TN = (((0,), (0,)), ((), ()))
NT = (((1,), (1,)), ((), ()))


def unit_rows(embedded):
    values = embedded.astype(F32)
    length = jnp.sqrt(jnp.sum(values * values, axis=1, keepdims=True) + 1e-06)
    inverse = 1.0 / length
    return (values * inverse).astype(BF16), inverse


def partial_kernel(
    n_chips,
    first_chip,
    pairs_total,
    place_ref,
    params_hbm,
    img_hbm,
    txt_hbm,
    feats_hbm,
    img_ids_hbm,
    txt_ids_hbm,
    mine_ref,
    other_ref,
    grads_ref,
    params_ref,
    img_ref,
    txt_ref,
    feats_ref,
    img_ids_ref,
    txt_ids_ref,
    sems,
):
    copies = []
    for number, (source, target) in enumerate(
        (
            (img_hbm, img_ref),
            (txt_hbm, txt_ref),
            (img_ids_hbm, img_ids_ref),
            (txt_ids_hbm, txt_ids_ref),
            (params_hbm, params_ref),
            (feats_hbm, feats_ref),
        )
    ):
        copies.append(pltpu.make_async_copy(source, target, sems.at[number]))
        copies[-1].start()
    rows = img_ref.shape[0]
    width = feats_ref.shape[1]
    pair = width // n_chips
    block = pair // 2
    body = block // 8 * 8
    n_tiles = (width + rows) // 128
    copies[0].wait()
    img_unit, img_inverse = unit_rows(img_ref[...])
    copies[1].wait()
    txt_unit, txt_inverse = unit_rows(txt_ref[...])
    for copy in copies[2:5]:
        copy.wait()
    scale_t = params_ref[0]
    shift_b = params_ref[1]
    factor = scale_t * (-params_ref[2] / pairs_total)
    similar = lax.dot_general(img_unit, txt_unit, NT, preferred_element_type=F32)
    logits = scale_t * similar + shift_b
    img_ids = jnp.broadcast_to(img_ids_ref[...], (8, rows)).T[:, 0:1]
    same = img_ids == txt_ids_ref[...]
    minus = jnp.where(same, logits, -logits)
    weights = (jnp.where(same, factor, -factor) / (1.0 + jnp.exp(minus))).astype(BF16)
    img_radial = jnp.sum(weights.astype(F32) * similar, axis=1, keepdims=True)
    img_grad = jnp.dot(weights, txt_unit, preferred_element_type=F32)
    img_grad = (img_grad - img_unit.astype(F32) * img_radial) * img_inverse
    grads_ref[:, width:] = img_grad.T
    txt_grad = lax.dot_general(weights, img_unit, TN, preferred_element_type=F32)
    txt_values = txt_unit.astype(F32)
    txt_radial = jnp.sum(txt_grad * txt_values, axis=1, keepdims=True)
    txt_grad = ((txt_grad - txt_values * txt_radial) * txt_inverse).astype(BF16)
    copies[5].wait()
    grads_ref[:, 0:width] = lax.dot_general(
        feats_ref[...], txt_grad, TN, preferred_element_type=F32
    )
    me = place_ref[0] % 2
    low_half = lax.broadcasted_iota(jnp.int32, (8, 128), 0) < 4
    for core in range(2):

        @pl.when(me == core)
        def _():
            for chip in range(n_chips):
                shared = grads_ref[pair * chip + body : pair * chip + body + 8, :]
                turned = pltpu.roll(shared, 4, 0)
                slot = (chip - first_chip) % n_chips
                for kept, ref in ((core, mine_ref), (1 - core, other_ref)):
                    start = pair * chip + (body + 8) * kept
                    whole = grads_ref[start : start + body, :].astype(ref.dtype)
                    even, odd = (turned, shared) if kept else (shared, turned)
                    for tile in range(n_tiles):
                        ref[slot, body * tile : body * (tile + 1), :] = whole[
                            :, 128 * tile : 128 * (tile + 1)
                        ]
                    ends = []
                    for tile in range(0, n_tiles, 2):
                        last = min(tile + 1, n_tiles - 1)
                        ends.append(
                            jnp.where(
                                low_half,
                                even[:, 128 * tile : 128 * (tile + 1)],
                                odd[:, 128 * last : 128 * (last + 1)],
                            )
                        )
                    ref[slot, body * n_tiles :, :] = jnp.concatenate(ends, axis=0).astype(ref.dtype)


def project_kernel(
    first_far,
    block,
    place_ref,
    parts_ref,
    feats_ref,
    mine_ref,
    other_ref,
    rows_ref,
    total_ref,
    blocks_ref,
):
    n_parts = parts_ref.shape[0]
    rows, width = feats_ref.shape
    body = block // 8 * 8
    n_tiles = (width + rows) // 128
    total = parts_ref[0].astype(F32)
    for part in range(1, n_parts):
        total = total + parts_ref[part].astype(F32)
    for tile in range(n_tiles):
        columns = slice(128 * tile, 128 * (tile + 1))
        total_ref[0:body, columns] = total[body * tile : body * (tile + 1)]
        start = body * n_tiles + 8 * (tile // 2)
        end = total[start : start + 8]
        total_ref[body : body + 8, columns] = pltpu.roll(end, 4, 0) if tile % 2 else end
    text = total_ref[0:block, 0:width]
    image = total_ref[:, width:]
    high = image.astype(BF16)
    low = (image - high.astype(F32)).astype(BF16)
    feats = feats_ref[...]
    projected = jnp.dot(high, feats, preferred_element_type=F32) + jnp.dot(
        low, feats, preferred_element_type=F32
    )
    both = jnp.concatenate(
        [projected[0:block], text, jnp.zeros((128 - 2 * block, width), F32)], axis=0
    )
    rows_ref[...] = both.T
    first = mine_ref.shape[1]
    n_near, n_far = blocks_ref.shape[0:2]
    rest = block - first
    lane = lax.broadcasted_iota(jnp.int32, (first, 128), 1)
    for target in range(n_far * n_near):
        top = rows_ref[target * block : target * block + first, :]
        bottom = rows_ref[target * block + first : (target + 1) * block, :]
        tail = jnp.concatenate(
            [pltpu.roll(bottom, 2 * block, 1), pltpu.roll(bottom, block, 1)], axis=0
        )
        place = (target // n_near - first_far) % n_far
        blocks_ref[target % n_near, place] = jnp.where(lane < 2 * block, top, tail)
    near = place_ref[0] // 2
    mine_ref[...] = blocks_ref[near]
    other_ref[...] = blocks_ref[1 - near].astype(other_ref.dtype)


def total_kernel(block, place_ref, parts_ref, img_ref, txt_ref):
    total = parts_ref[0].astype(F32)
    for part in range(1, parts_ref.shape[0]):
        total = total + parts_ref[part].astype(F32)
    first = parts_ref.shape[1]
    rest = block - first
    extra = block % 8
    image_bottom = pltpu.roll(total, 128 - 2 * block, 1)[0:rest]
    text_bottom = pltpu.roll(total, 128 - block, 1)[rest : 2 * rest]
    lane = lax.broadcasted_iota(jnp.int32, (rest, 128), 1)
    bottom = jnp.where(lane < block, image_bottom, text_bottom)
    whole = jnp.concatenate([total, bottom, jnp.zeros((128 - block, 128), F32)], axis=0)
    place = lax.broadcasted_iota(jnp.int32, whole.shape, 1)
    inside = jnp.where(place < block, place, place - block)
    ordered = jnp.where(
        inside < extra, pltpu.roll(whole, 128 - (block - extra), 1), pltpu.roll(whole, extra, 1)
    )
    whole = jnp.where(place_ref[0] % 2 == 1, ordered, whole)
    img_ref[...] = whole[0:block, 0:block]
    txt_ref[...] = whole.T[block : 2 * block, 0:block]


def whole_spec():
    return pl.BlockSpec(memory_space=pltpu.VMEM)


def scalar_spec():
    return pl.BlockSpec(memory_space=pltpu.SMEM)


def compiler_params(mib):
    return pltpu.CompilerParams(vmem_limit_bytes=mib * 1024 * 1024)


def turned(size, first):
    return [(first + number) % size for number in range(size)]


def per_device(img_embed, txt_embed, img_feats, txt_feats, img_ids, txt_ids, loss_params):
    n_far, n_near = lax.axis_size("far"), lax.axis_size("near")
    n_loop = n_far * n_near
    n_chips = lax.axis_size("chip")
    rows, width = img_embed.shape
    block = width // n_loop
    first_chip = n_chips // 2 + n_chips // 8
    place = lax.axis_index(("near", "core")).astype(jnp.int32).reshape(1)
    lanes = width + rows
    shape = (n_chips, -(-block * (lanes // 128) // 8) * 8, 128)
    mine, other = pl.pallas_call(
        functools.partial(partial_kernel, n_chips, first_chip, float(rows * n_loop)),
        out_shape=(jax.ShapeDtypeStruct(shape, F32), jax.ShapeDtypeStruct(shape, BF16)),
        in_specs=[scalar_spec()] + [pl.BlockSpec(memory_space=pltpu.HBM)] * 6,
        out_specs=[whole_spec()] * 2,
        scratch_shapes=[
            pltpu.VMEM((width, lanes), F32),
            pltpu.SMEM(loss_params.shape, F32),
            pltpu.VMEM(img_embed.shape, BF16),
            pltpu.VMEM(txt_embed.shape, BF16),
            pltpu.VMEM(txt_feats.shape, BF16),
            pltpu.VMEM((1, rows), jnp.int32),
            pltpu.VMEM((1, txt_ids.shape[0]), jnp.int32),
            pltpu.SemaphoreType.DMA((6,)),
        ],
        compiler_params=compiler_params(36),
        name="partial_gradients",
    )(
        place,
        *(
            pltpu.with_memory_space_constraint(array, pltpu.HBM)
            for array in (
                loss_params,
                img_embed,
                txt_embed,
                txt_feats,
                img_ids.reshape(1, rows),
                txt_ids.reshape(1, -1),
            )
        ),
    )
    theirs = lax.ppermute(other, "core", [(0, 1), (1, 0)])
    chip_sum = (mine + theirs.astype(F32)).astype(BF16)
    parts = lax.all_to_all(
        chip_sum,
        "chip",
        split_axis=0,
        concat_axis=0,
        axis_index_groups=[turned(n_chips, first_chip)],
        tiled=True,
    )
    first_far = n_far // 2
    shape = (n_far, 2 * block // 3, 128)
    mine, other = pl.pallas_call(
        functools.partial(project_kernel, first_far, block),
        out_shape=(jax.ShapeDtypeStruct(shape, F32), jax.ShapeDtypeStruct(shape, BF16)),
        in_specs=[scalar_spec()] + [whole_spec()] * 2,
        out_specs=[whole_spec()] * 2,
        scratch_shapes=[
            pltpu.VMEM((width, 128), F32),
            pltpu.VMEM((block // 8 * 8 + 8, lanes), F32),
            pltpu.VMEM((n_near,) + shape, F32),
        ],
        compiler_params=compiler_params(16),
        name="project_blocks",
    )(place, parts, img_feats)
    theirs = lax.ppermute(other, "near", [(0, 1), (1, 0)])
    near_sum = (mine + theirs.astype(F32)).astype(BF16)
    loop_parts = lax.all_to_all(
        near_sum, "far", split_axis=0, concat_axis=0, axis_index_groups=[turned(n_far, first_far)], tiled=True
    )
    return pl.pallas_call(
        functools.partial(total_kernel, block),
        out_shape=(jax.ShapeDtypeStruct((block, block), F32),) * 2,
        in_specs=[scalar_spec(), whole_spec()],
        out_specs=[whole_spec()] * 2,
        compiler_params=compiler_params(4),
        name="sum_blocks",
    )(place, loop_parts)


def solution(mesh):
    shape = mesh.shape
    near = 2
    sizes = (shape["dp"] // near, near, shape["dom"] * shape["mp"] // 2, 2)
    mesh = Mesh(np.asarray(mesh.devices).reshape(sizes), ("far", "near", "chip", "core"))
    loop = ("far", "near")
    plane = ("chip", "core")
    return jax.shard_map(
        per_device,
        mesh=mesh,
        in_specs=(
            P(loop, None),
            P(plane, None),
            P(loop, None),
            P(plane, None),
            P(loop),
            P(plane),
            P(),
        ),
        out_specs=(P(loop, plane), P(plane, loop)),
        check_vma=False,
    )
```

```python
import functools

import jax
import jax.numpy as jnp
import numpy as np
from jax import lax
from jax.experimental import pallas as pl
from jax.experimental.pallas import tpu as pltpu
from jax.sharding import Mesh
from jax.sharding import PartitionSpec as P

F32 = jnp.float32
BF16 = jnp.bfloat16
TN = (((0,), (0,)), ((), ()))
NT = (((1,), (1,)), ((), ()))


def unit_rows(embedded):
    values = embedded.astype(F32)
    length = jnp.sqrt(jnp.sum(values * values, axis=1, keepdims=True) + 1e-06)
    inverse = 1.0 / length
    return (values * inverse).astype(BF16), inverse


def partial_kernel(
    n_chips,
    first_chip,
    pairs_total,
    place_ref,
    params_hbm,
    img_hbm,
    txt_hbm,
    feats_hbm,
    img_ids_hbm,
    txt_ids_hbm,
    mine_ref,
    other_ref,
    grads_ref,
    params_ref,
    img_ref,
    txt_ref,
    feats_ref,
    img_ids_ref,
    txt_ids_ref,
    sems,
):
    copies = []
    for number, (source, target) in enumerate(
        (
            (img_hbm, img_ref),
            (txt_hbm, txt_ref),
            (img_ids_hbm, img_ids_ref),
            (txt_ids_hbm, txt_ids_ref),
            (params_hbm, params_ref),
            (feats_hbm, feats_ref),
        )
    ):
        copies.append(pltpu.make_async_copy(source, target, sems.at[number]))
        copies[-1].start()
    rows = img_ref.shape[0]
    width = feats_ref.shape[1]
    pair = width // n_chips
    block = pair // 2
    body = block // 8 * 8
    n_tiles = (width + rows) // 128
    copies[0].wait()
    img_unit, img_inverse = unit_rows(img_ref[...])
    copies[1].wait()
    txt_unit, txt_inverse = unit_rows(txt_ref[...])
    for copy in copies[2:5]:
        copy.wait()
    scale_t = params_ref[0]
    shift_b = params_ref[1]
    factor = scale_t * (-params_ref[2] / pairs_total)
    similar = lax.dot_general(img_unit, txt_unit, NT, preferred_element_type=F32)
    logits = scale_t * similar + shift_b
    img_ids = jnp.broadcast_to(img_ids_ref[...], (8, rows)).T[:, 0:1]
    same = img_ids == txt_ids_ref[...]
    minus = jnp.where(same, logits, -logits)
    weights = (jnp.where(same, factor, -factor) / (1.0 + jnp.exp(minus))).astype(BF16)
    img_radial = jnp.sum(weights.astype(F32) * similar, axis=1, keepdims=True)
    img_grad = jnp.dot(weights, txt_unit, preferred_element_type=F32)
    img_grad = (img_grad - img_unit.astype(F32) * img_radial) * img_inverse
    grads_ref[:, width:] = img_grad.T
    txt_grad = lax.dot_general(weights, img_unit, TN, preferred_element_type=F32)
    txt_values = txt_unit.astype(F32)
    txt_radial = jnp.sum(txt_grad * txt_values, axis=1, keepdims=True)
    txt_grad = ((txt_grad - txt_values * txt_radial) * txt_inverse).astype(BF16)
    copies[5].wait()
    grads_ref[:, 0:width] = lax.dot_general(
        feats_ref[...], txt_grad, TN, preferred_element_type=F32
    )
    me = place_ref[0] % 2
    low_half = lax.broadcasted_iota(jnp.int32, (8, 128), 0) < 4
    for core in range(2):

        @pl.when(me == core)
        def _():
            for chip in range(n_chips):
                shared = grads_ref[pair * chip + body : pair * chip + body + 8, :]
                turned = pltpu.roll(shared, 4, 0)
                slot = (chip - first_chip) % n_chips
                for kept, ref in ((core, mine_ref), (1 - core, other_ref)):
                    start = pair * chip + (body + 8) * kept
                    whole = grads_ref[start : start + body, :].astype(ref.dtype)
                    even, odd = (turned, shared) if kept else (shared, turned)
                    for tile in range(n_tiles):
                        ref[slot, body * tile : body * (tile + 1), :] = whole[
                            :, 128 * tile : 128 * (tile + 1)
                        ]
                    ends = []
                    for tile in range(0, n_tiles, 2):
                        last = min(tile + 1, n_tiles - 1)
                        ends.append(
                            jnp.where(
                                low_half,
                                even[:, 128 * tile : 128 * (tile + 1)],
                                odd[:, 128 * last : 128 * (last + 1)],
                            )
                        )
                    ref[slot, body * n_tiles :, :] = jnp.concatenate(ends, axis=0).astype(ref.dtype)


def project_kernel(
    first_far,
    block,
    place_ref,
    parts_ref,
    feats_ref,
    mine_ref,
    rows_ref,
    total_ref,
    blocks_ref,
):
    n_parts = parts_ref.shape[0]
    rows, width = feats_ref.shape
    body = block // 8 * 8
    n_tiles = (width + rows) // 128
    total = parts_ref[0].astype(F32)
    for part in range(1, n_parts):
        total = total + parts_ref[part].astype(F32)
    for tile in range(n_tiles):
        columns = slice(128 * tile, 128 * (tile + 1))
        total_ref[0:body, columns] = total[body * tile : body * (tile + 1)]
        start = body * n_tiles + 8 * (tile // 2)
        end = total[start : start + 8]
        total_ref[body : body + 8, columns] = pltpu.roll(end, 4, 0) if tile % 2 else end
    text = total_ref[0:block, 0:width]
    image = total_ref[:, width:]
    high = image.astype(BF16)
    low = (image - high.astype(F32)).astype(BF16)
    feats = feats_ref[...]
    projected = jnp.dot(high, feats, preferred_element_type=F32) + jnp.dot(
        low, feats, preferred_element_type=F32
    )
    both = jnp.concatenate(
        [projected[0:block], text, jnp.zeros((128 - 2 * block, width), F32)], axis=0
    )
    rows_ref[...] = both.T
    first = mine_ref.shape[2]
    n_near, n_far = blocks_ref.shape[0:2]
    rest = block - first
    lane = lax.broadcasted_iota(jnp.int32, (first, 128), 1)
    for target in range(n_far * n_near):
        top = rows_ref[target * block : target * block + first, :]
        bottom = rows_ref[target * block + first : (target + 1) * block, :]
        tail = jnp.concatenate(
            [pltpu.roll(bottom, 2 * block, 1), pltpu.roll(bottom, block, 1)], axis=0
        )
        place = (target // n_near - first_far) % n_far
        blocks_ref[target % n_near, place] = jnp.where(lane < 2 * block, top, tail)
    mine_ref[...] = blocks_ref[...].astype(mine_ref.dtype)


def total_kernel(block, place_ref, parts_ref, img_ref, txt_ref):
    total = parts_ref[0].astype(F32)
    for part in range(1, parts_ref.shape[0]):
        total = total + parts_ref[part].astype(F32)
    first = parts_ref.shape[1]
    rest = block - first
    extra = block % 8
    image_bottom = pltpu.roll(total, 128 - 2 * block, 1)[0:rest]
    text_bottom = pltpu.roll(total, 128 - block, 1)[rest : 2 * rest]
    lane = lax.broadcasted_iota(jnp.int32, (rest, 128), 1)
    bottom = jnp.where(lane < block, image_bottom, text_bottom)
    whole = jnp.concatenate([total, bottom, jnp.zeros((128 - block, 128), F32)], axis=0)
    place = lax.broadcasted_iota(jnp.int32, whole.shape, 1)
    inside = jnp.where(place < block, place, place - block)
    ordered = jnp.where(
        inside < extra, pltpu.roll(whole, 128 - (block - extra), 1), pltpu.roll(whole, extra, 1)
    )
    whole = jnp.where(place_ref[0] % 2 == 1, ordered, whole)
    img_ref[...] = whole[0:block, 0:block]
    txt_ref[...] = whole.T[block : 2 * block, 0:block]


def whole_spec():
    return pl.BlockSpec(memory_space=pltpu.VMEM)


def scalar_spec():
    return pl.BlockSpec(memory_space=pltpu.SMEM)


def compiler_params(mib):
    return pltpu.CompilerParams(vmem_limit_bytes=mib * 1024 * 1024)


def turned(size, first):
    return [(first + number) % size for number in range(size)]


def per_device(img_embed, txt_embed, img_feats, txt_feats, img_ids, txt_ids, loss_params):
    n_far, n_near = lax.axis_size("far"), lax.axis_size("near")
    n_loop = n_far * n_near
    n_chips = lax.axis_size("chip")
    rows, width = img_embed.shape
    block = width // n_loop
    first_chip = n_chips // 2 + n_chips // 8
    place = lax.axis_index(("near", "core")).astype(jnp.int32).reshape(1)
    lanes = width + rows
    shape = (n_chips, -(-block * (lanes // 128) // 8) * 8, 128)
    mine, other = pl.pallas_call(
        functools.partial(partial_kernel, n_chips, first_chip, float(rows * n_loop)),
        out_shape=(jax.ShapeDtypeStruct(shape, F32), jax.ShapeDtypeStruct(shape, BF16)),
        in_specs=[scalar_spec()] + [pl.BlockSpec(memory_space=pltpu.HBM)] * 6,
        out_specs=[whole_spec()] * 2,
        scratch_shapes=[
            pltpu.VMEM((width, lanes), F32),
            pltpu.SMEM(loss_params.shape, F32),
            pltpu.VMEM(img_embed.shape, BF16),
            pltpu.VMEM(txt_embed.shape, BF16),
            pltpu.VMEM(txt_feats.shape, BF16),
            pltpu.VMEM((1, rows), jnp.int32),
            pltpu.VMEM((1, txt_ids.shape[0]), jnp.int32),
            pltpu.SemaphoreType.DMA((6,)),
        ],
        compiler_params=compiler_params(36),
        name="partial_gradients",
    )(
        place,
        *(
            pltpu.with_memory_space_constraint(array, pltpu.HBM)
            for array in (
                loss_params,
                img_embed,
                txt_embed,
                txt_feats,
                img_ids.reshape(1, rows),
                txt_ids.reshape(1, -1),
            )
        ),
    )
    theirs = lax.ppermute(other, "core", [(0, 1), (1, 0)])
    chip_sum = (mine + theirs.astype(F32)).astype(BF16)
    parts = lax.all_to_all(
        chip_sum,
        "chip",
        split_axis=0,
        concat_axis=0,
        axis_index_groups=[turned(n_chips, first_chip)],
        tiled=True,
    )
    first_far = n_far // 2
    shape = (n_far, 2 * block // 3, 128)
    blocks = pl.pallas_call(
        functools.partial(project_kernel, first_far, block),
        out_shape=jax.ShapeDtypeStruct((n_near,) + shape, BF16),
        in_specs=[scalar_spec()] + [whole_spec()] * 2,
        out_specs=whole_spec(),
        scratch_shapes=[
            pltpu.VMEM((width, 128), F32),
            pltpu.VMEM((block // 8 * 8 + 8, lanes), F32),
            pltpu.VMEM((n_near,) + shape, F32),
        ],
        compiler_params=compiler_params(16),
        name="project_blocks",
    )(place, parts, img_feats)
    near_parts = lax.all_to_all(blocks, "near", split_axis=0, concat_axis=0, tiled=True)
    near_sum = jnp.sum(near_parts.astype(F32), axis=0).astype(BF16)
    loop_parts = lax.all_to_all(
        near_sum, "far", split_axis=0, concat_axis=0, axis_index_groups=[turned(n_far, first_far)], tiled=True
    )
    return pl.pallas_call(
        functools.partial(total_kernel, block),
        out_shape=(jax.ShapeDtypeStruct((block, block), F32),) * 2,
        in_specs=[scalar_spec(), whole_spec()],
        out_specs=[whole_spec()] * 2,
        compiler_params=compiler_params(4),
        name="sum_blocks",
    )(place, loop_parts)


def solution(mesh):
    shape = mesh.shape
    near = 4
    sizes = (shape["dp"] // near, near, shape["dom"] * shape["mp"] // 2, 2)
    mesh = Mesh(np.asarray(mesh.devices).reshape(sizes), ("far", "near", "chip", "core"))
    loop = ("far", "near")
    plane = ("chip", "core")
    return jax.shard_map(
        per_device,
        mesh=mesh,
        in_specs=(
            P(loop, None),
            P(plane, None),
            P(loop, None),
            P(plane, None),
            P(loop),
            P(plane),
            P(),
        ),
        out_specs=(P(loop, plane), P(plane, loop)),
        check_vma=False,
    )
```
